32 devices in a mesh: groups: 2 (over y), region: 4 (over z), head: 4 (over x, core).
Axes of the slice: x: 2, y: 2, z: 4, core: 2. Of those that a mesh axis runs over, the one named last changes fastest.
Arguments:
- video_queries: bfloat16 [2, 4, 256, 3072], P('groups', 'region', None, 'head'), parts along dimension 0, may hold values from -6 to 6
- video_keys: bfloat16 [2, 4, 256, 3072], P('groups', 'region', None, 'head'), parts along dimension 0, may hold values from -6 to 6
- video_values: bfloat16 [2, 4, 256, 3072], P('groups', 'region', None, 'head'), parts along dimension 0, may hold values from -12 to 12
- head_window: int32 [24, 2], P('head'), may hold values from 0 to 1
- prompt_keys: bfloat16 [512, 3072], P(('groups', 'region'), 'head'), parts along dimension 0, may hold values from -10 to 10
- prompt_values: bfloat16 [512, 3072], P(('groups', 'region'), 'head'), parts along dimension 0, may hold values from -10 to 10
- text_len: int32 [2], P('groups'), parts along dimension 0, may hold values from 64 to 256
Outputs:
- attended: bfloat16 [2, 4, 256, 3072], P('groups', 'region', None, 'head'), parts along dimension 0
The draws below stay inside these ranges and needn't reach their ends.
There are 2 independent parts, one for each index of `groups`. The reference program is written for one: setup_inputs(seed, part) draws one part's arguments, and reference() takes and returns one part's arrays. A program takes and returns all parts, laid end to end along the dimension named above; an argument that names none is the same for every part. Nothing has to cross between parts.
Inputs may be any that keep to these rules, and one draw needn't show every extreme that they name: `head_window`: entry (h, 0) is head h's reach in tiles along grid rows, (h, 1) along grid columns; the window spans 2 r + 1 tiles along each. The first text_len[0] of the 256 prompt tokens are live.
All inputs are finite; a program needn't handle non-finite values.
Results may differ from the reference program's by a relative error of at most 0.0035.
Values may be sent and summed in bfloat16 or wider, within the bound.
No kernel may reach another device: no remote copies, remote signals or barrier semaphores. Data moves between devices by JAX's collectives and lax.ppermute only.
A program may use at most 128 MiB of HBM per device.

```python
import math
import jax
import jax.numpy as jnp
from jax import lax

HEADS = 24
HEAD_DIM = 128
TEXT = 256
SLABS = 1
TILE_TOK = 256
DEV_COLS = 2
GRID_ROWS = 2
TILES = 4


def draw_entries(key):
    streams = jax.random.split(jax.random.fold_in(key, 4211), 2)
    array_shape = (SLABS, TILES, TILE_TOK, HEADS * HEAD_DIM)
    queries = 1.5 * jax.random.truncated_normal(streams[0], -4.0, 4.0, array_shape, jnp.float32)
    keys_drawn = 1.5 * jax.random.truncated_normal(streams[1], -4.0, 4.0, array_shape, jnp.float32)
    return (queries, keys_drawn)


def draw_video_queries(key, part):
    return draw_entries(key)[0].astype(jnp.bfloat16)


def draw_video_keys(key, part):
    return draw_entries(key)[1].astype(jnp.bfloat16)


def plant(values, key, low, largest):
    longest = values.shape.index(max(values.shape))
    spots = []
    for shift in (0, 1):
        where = [jax.random.randint(jax.random.fold_in(key, axis), (), 0, length) for axis, length in enumerate(values.shape)]
        where[longest] = (where[longest] + shift) % values.shape[longest]
        spots.append(tuple(where))
    return values.at[spots[0]].set(low).at[spots[1]].set(largest)


def shard_levels(stream_key, dims, shards, low, high):
    def one(dim, parts):
        heights = jax.random.uniform(jax.random.fold_in(jax.random.fold_in(stream_key, 6), dim), (parts,), jnp.float32, low / len(shards), high / len(shards))
        return jnp.repeat(jnp.exp(heights), dims[dim] // parts).reshape((-1,) + (1,) * (len(dims) - dim - 1))

    level = one(*shards[0])
    for cut in shards[1:]:
        level = level * one(*cut)
    return level


def centred(own_key, extent, width, most, pieces=(), kind=jnp.bfloat16):
    gain = shard_levels(own_key, extent, pieces, -0.22, 0.18) if pieces else 1.0
    drawn = jax.random.normal(own_key, extent, jnp.float32) * width * gain
    return jnp.minimum(jnp.maximum(drawn, -most), most).astype(kind)


def setup_inputs(seed: int = 0, part: int = 0) -> dict:
    key_of = jax.random.split(jax.random.key(seed), 8)
    part_splits = jax.random.split(jax.random.fold_in(key_of[7], part), 8)
    video_queries = draw_video_queries(jax.random.fold_in(jax.random.fold_in(key_of[7], part), 71), part)
    video_keys = draw_video_keys(jax.random.fold_in(jax.random.fold_in(key_of[7], part), 71), part)
    video_values = centred(part_splits[2], (SLABS, TILES, TILE_TOK, HEADS * HEAD_DIM), 2.0, 12.0, ((1, 4), (3, 4)))
    head_window = plant(jax.random.randint(key_of[3], (HEADS, 2), 0, 2), jax.random.fold_in(key_of[3], 1), 0, 1).astype(jnp.int32)
    prompt_keys = centred(part_splits[4], (TEXT, HEADS * HEAD_DIM), 2.0, 10.0, ((0, 4), (1, 4)))
    prompt_values = centred(part_splits[5], (TEXT, HEADS * HEAD_DIM), 2.0, 10.0, ((0, 4), (1, 4)))
    text_len = jax.random.randint(part_splits[6], (1,), TEXT // 4, TEXT + 1).astype(jnp.int32)
    return dict(video_queries=video_queries, video_keys=video_keys, video_values=video_values, head_window=head_window, prompt_keys=prompt_keys, prompt_values=prompt_values, text_len=text_len)


def reference(video_queries, video_keys, video_values, head_window, prompt_keys, prompt_values, text_len):
    score_scale = 1.0 / math.sqrt(HEAD_DIM)

    def heads_first(array_in):
        array_in = array_in.astype(jnp.float32).reshape(SLABS, GRID_ROWS, DEV_COLS, TILE_TOK, HEADS, HEAD_DIM)
        return jnp.transpose(array_in, (4, 0, 1, 2, 3, 5))

    def prompt_heads(array_in):
        return jnp.transpose(array_in.astype(jnp.float32).reshape(TEXT, HEADS, HEAD_DIM), (1, 0, 2))
    row_ids = jnp.arange(GRID_ROWS, dtype=jnp.int32)[:, None]
    col_ids = jnp.arange(DEV_COLS, dtype=jnp.int32)[None, :]
    text_live = jnp.arange(TEXT, dtype=jnp.int32) < text_len[0]

    def one_head(head_item):
        head_queries, head_keys, head_values, text_keys, text_values, head_reach = head_item
        padding = ((0, 0), (1, 1), (1, 1), (0, 0), (0, 0))
        padded_keys = jnp.pad(head_keys, padding)
        padded_values = jnp.pad(head_values, padding)
        key_list, value_list, live_list = ([], [], [])
        for row_step in (-1, 0, 1):
            for col_step in (-1, 0, 1):
                key_list.append(padded_keys[:, 1 + row_step:1 + row_step + GRID_ROWS, 1 + col_step:1 + col_step + DEV_COLS])
                value_list.append(padded_values[:, 1 + row_step:1 + row_step + GRID_ROWS, 1 + col_step:1 + col_step + DEV_COLS])
                inside = (row_ids + row_step >= 0) & (row_ids + row_step < GRID_ROWS) & (col_ids + col_step >= 0) & (col_ids + col_step < DEV_COLS)
                within = (abs(row_step) <= head_reach[0]) & (abs(col_step) <= head_reach[1])
                live_list.append(inside & within)
        near_keys = jnp.concatenate(key_list, axis=3)
        near_values = jnp.concatenate(value_list, axis=3)
        near_live = jnp.repeat(jnp.stack(live_list, axis=2), TILE_TOK, axis=2)
        near_scores = jnp.einsum('srcqd,srckd->srcqk', head_queries, near_keys) * score_scale
        near_scores = jnp.where(near_live[None, :, :, None, :], near_scores, -jnp.inf)
        text_scores = jnp.einsum('srcqd,kd->srcqk', head_queries, text_keys) * score_scale
        text_scores = jnp.where(text_live, text_scores, -jnp.inf)
        scores = jnp.concatenate([near_scores, text_scores], axis=-1)
        row_max = lax.optimization_barrier(jnp.max(scores, axis=-1, keepdims=True))
        weights = jnp.exp(scores - row_max)
        row_sum = lax.optimization_barrier(jnp.sum(weights, axis=-1, keepdims=True))
        rounded = lax.optimization_barrier(weights.astype(jnp.bfloat16)).astype(jnp.float32)
        split_at = 9 * TILE_TOK
        summed = jnp.einsum('srcqk,srckd->srcqd', rounded[..., :split_at], near_values)
        summed = summed + jnp.einsum('srcqk,kd->srcqd', rounded[..., split_at:], text_values)
        return summed / row_sum
    per_head = lax.map(one_head, (heads_first(video_queries), heads_first(video_keys), heads_first(video_values), prompt_heads(prompt_keys), prompt_heads(prompt_values), head_window))
    per_head = jnp.transpose(per_head, (1, 2, 3, 4, 0, 5)).reshape(SLABS, TILES, TILE_TOK, HEADS * HEAD_DIM)
    return per_head.astype(jnp.bfloat16)
```

```python
import functools
import math

import jax
import jax.numpy as jnp
from jax import lax
from jax.experimental import pallas as pl
from jax.experimental.pallas import tpu as pltpu
from jax.sharding import PartitionSpec as P

VMEM = pl.BlockSpec(memory_space=pltpu.VMEM)
SMEM = pl.BlockSpec(memory_space=pltpu.SMEM)
KINDS = ((1, 0), (1, 1), (0, 1), (0, 0))


def counts_of(head_count):
    span = range(head_count + 1)
    return [
        (rows, both, cols)
        for rows in span
        for both in span[: head_count - rows + 1]
        for cols in span[: head_count - rows - both + 1]
    ]


def runs_of(rows, both, cols):
    return {(1, 0): (0, rows + both), (0, 1): (rows, rows + both + cols), (1, 1): (rows, rows + both)}


def pack_kernel(pack_first, window, keys, values, prompt_keys, prompt_values, packed, prompts, meta):
    head_count = window.shape[0]
    head_dim = keys.shape[1] // head_count
    prompts[0] = prompt_keys[...]
    prompts[1] = prompt_values[...]
    kinds = []
    for head in range(head_count):
        rows, cols = window[head, 0], window[head, 1]
        kinds.append(jnp.where(rows > 0, jnp.where(cols > 0, 1, 0), jnp.where(cols > 0, 2, 3)))
    totals = [sum((kind == value).astype(jnp.int32) for kind in kinds) for value in range(3)]
    for head in range(head_count):
        slot = jnp.int32(0)
        for other in range(head_count):
            if other != head:
                ahead = kinds[other] <= kinds[head] if other < head else kinds[other] < kinds[head]
                slot = slot + ahead.astype(jnp.int32)
        meta[slot] = jnp.int32(head)
        meta[head_count + slot] = kinds[head]
        columns = slice(head * head_dim, (head + 1) * head_dim)
        packed[slot, 0] = keys[:, columns]
        packed[slot, 1] = values[:, columns]
    rows, both, cols = totals
    rank = cols
    for step in range(head_count):
        left = head_count - step
        rank = rank + jnp.where(step < rows, (left + 1) * (left + 2) // 2, 0)
        rank = rank + jnp.where(step < both, left - rows + 1, 0)
    meta[2 * head_count] = rank
    meta[2 * head_count + 1] = rows if pack_first else jnp.int32(0)


def attend_kernel(moves, grid_shape, order, meta, text_len, queries, keys, values, *rest):
    *blocks, out = rest
    arrived, prompts = blocks[: len(moves)], blocks[len(moves) :]
    head_count = arrived[0].shape[0]
    tile_tok = keys.shape[0]
    head_dim = keys.shape[1] // head_count
    scale = 1.0 / math.sqrt(head_dim)
    position = lax.axis_index("region")
    row, col = position // grid_shape[1], position % grid_shape[1]
    nothing = jnp.float32(-1e30)
    biases = []
    for block, owner in zip(prompts, order):
        held = block.shape[1]
        first = owner(position) * held
        tokens = first + lax.broadcasted_iota(jnp.int32, (1, held), 1)
        biases.append(jnp.where(tokens < text_len[0], jnp.float32(0), nothing))
    prompt_bias = jnp.concatenate(biases, axis=1)

    def one_slot(slot, carry):
        head = meta[slot]
        kind = meta[head_count + slot]
        columns = pl.ds(pl.multiple_of(head * head_dim, head_dim), head_dim)

        for number, reach in enumerate(KINDS):
            @pl.when(kind == number)
            def _():
                key_list = [keys[:, columns]]
                value_list = [values[:, columns]]
                bias_list = [jnp.zeros((1, tile_tok), jnp.float32)]
                for block, (row_step, col_step) in zip(arrived, moves):
                    if abs(row_step) <= reach[0] and abs(col_step) <= reach[1]:
                        use = slot
                        if not (row_step and not col_step):
                            use = slot - meta[2 * head_count + 1]
                        key_list.append(block[use, 0])
                        value_list.append(block[use, 1])
                        bias = jnp.zeros((1, tile_tok), jnp.float32)
                        if grid_shape != (2, 2):
                            from_row, from_col = row - row_step, col - col_step
                            there = (from_row >= 0) & (from_row < grid_shape[0])
                            there = there & (from_col >= 0) & (from_col < grid_shape[1])
                            bias = bias + jnp.where(there, jnp.float32(0), nothing)
                        bias_list.append(bias)
                for block in prompts:
                    key_list.append(block[0, :, columns])
                    value_list.append(block[1, :, columns])
                all_keys = jnp.concatenate(key_list, axis=0)
                all_values = jnp.concatenate(value_list, axis=0)
                bias = jnp.concatenate(bias_list + [prompt_bias], axis=1)
                scores = lax.dot_general(
                    queries[:, columns], all_keys, (((1,), (1,)), ((), ())),
                    preferred_element_type=jnp.float32,
                )
                scores = scores * scale + bias
                row_max = jnp.max(scores, axis=1, keepdims=True)
                weights = jnp.exp(scores - row_max)
                row_sum = jnp.sum(weights, axis=1, keepdims=True)
                attended = jnp.dot(
                    weights.astype(jnp.bfloat16), all_values, preferred_element_type=jnp.float32
                )
                out[:, columns] = (attended / row_sum).astype(out.dtype)

        return carry

    lax.fori_loop(0, head_count, one_slot, 0)


def shards(
    video_queries, video_keys, video_values, head_window, prompt_keys, prompt_values, text_len
):
    tile_shape = video_queries.shape[2:]
    tile_tok, features = tile_shape
    head_count = head_window.shape[0]
    head_dim = features // head_count
    region_count = lax.axis_size("region")
    grid_cols = min(8, region_count // 2)
    grid_shape = (region_count // grid_cols, grid_cols)
    queries = video_queries.reshape(tile_shape)
    keys = video_keys.reshape(tile_shape)
    values = video_values.reshape(tile_shape)

    def steps(extent):
        return (0, 1) if extent == 2 else (0, 1, -1)

    moves = [(r, c) for r in steps(grid_shape[0]) for c in steps(grid_shape[1]) if r or c]

    def pairs(move):
        links = []
        for source in range(region_count):
            place = [source // grid_cols + move[0], source % grid_cols + move[1]]
            for axis in range(2):
                if grid_shape[axis] == 2:
                    place[axis] %= 2
            if 0 <= place[0] < grid_shape[0] and 0 <= place[1] < grid_cols:
                links.append((source, place[0] * grid_cols + place[1]))
        return links

    small = grid_shape == (2, 2)
    packed, prompt_own, meta = pl.pallas_call(
        functools.partial(pack_kernel, small),
        out_shape=(
            jax.ShapeDtypeStruct((head_count, 2, tile_tok, head_dim), keys.dtype),
            jax.ShapeDtypeStruct((2,) + prompt_keys.shape, prompt_keys.dtype),
            jax.ShapeDtypeStruct((2 * head_count + 2,), jnp.int32),
        ),
        in_specs=[SMEM, VMEM, VMEM, VMEM, VMEM],
        out_specs=(VMEM, VMEM, SMEM),
    )(head_window, keys, values, prompt_keys, prompt_values)

    def exchange(count, packed, prompt_own):
        arrived = []
        if small:
            across_rows = lax.ppermute(prompt_own, "region", pairs((1, 0)))
            across_cols = lax.ppermute(prompt_own, "region", pairs((0, 1)))
            across_both = lax.ppermute(across_rows, "region", pairs((0, 1)))
            prompts = (prompt_own, across_cols, across_rows, across_both)
        else:
            prompts = (lax.all_gather(prompt_own, "region", axis=1, tiled=True),)
        for move in moves:
            first, last = runs_of(*count)[(abs(move[0]), abs(move[1]))]
            if first == last:
                arrived.append(jnp.zeros_like(packed))
                continue
            got = lax.ppermute(packed[first:last], "region", pairs(move))
            arrived.append(jnp.pad(got, ((0, head_count - last + first), (0, 0), (0, 0), (0, 0))))
        return tuple(arrived), prompts

    counts = counts_of(head_count)
    if small:
        arrived, prompts = lax.switch(
            meta[2 * head_count],
            [functools.partial(exchange, count) for count in counts],
            packed,
            prompt_own,
        )
        order = tuple((lambda z, k=k: z ^ k) for k in range(region_count))
    else:
        arrived, prompts = exchange((0, head_count, 0), packed, prompt_own)
        order = (lambda z: 0,)

    result = pl.pallas_call(
        functools.partial(attend_kernel, moves, grid_shape, order),
        out_shape=jax.ShapeDtypeStruct(tile_shape, video_queries.dtype),
        in_specs=[SMEM, SMEM] + [VMEM] * (3 + len(arrived) + len(prompts)),
        out_specs=VMEM,
        compiler_params=pltpu.CompilerParams(vmem_limit_bytes=40 * 1024 * 1024),
    )(meta, text_len, queries, keys, values, *arrived, *prompts)
    return result.reshape(video_queries.shape)


def solution(mesh):
    in_specs = (
        P("groups", "region", None, "head"),
        P("groups", "region", None, "head"),
        P("groups", "region", None, "head"),
        P("head", None),
        P(("groups", "region"), "head"),
        P(("groups", "region"), "head"),
        P("groups"),
    )
    out_specs = P("groups", "region", None, "head")
    return jax.shard_map(shards, mesh=mesh, in_specs=in_specs, out_specs=out_specs, check_vma=False)
```

```python
import functools
import math

import jax
import jax.numpy as jnp
import numpy as np
from jax import lax
from jax.experimental import pallas as pl
from jax.experimental.pallas import tpu as pltpu
from jax.sharding import PartitionSpec as P

VMEM = pl.BlockSpec(memory_space=pltpu.VMEM)
SMEM = pl.BlockSpec(memory_space=pltpu.SMEM)
KINDS = ((1, 1), (0, 1), (0, 0), (1, 0))
LEAVES = 24


def send_sizes(head_count, wanted):
    span = range(head_count + 1)
    cases, chance = [], []
    for both in span:
        for cols in span[: head_count - both + 1]:
            for rows in span[: head_count - both - cols + 1]:
                parts = (both, cols, rows, head_count - both - cols - rows)
                cases.append((both, both + cols, rows))
                chance.append(1.0 / math.prod(math.factorial(part) for part in parts))

    def cost(sizes):
        middle = 4 * (sizes[0] + sizes[2])
        outer = 2 * (2 * sizes[0] + sizes[1] + sizes[2])
        return max(middle, outer) + 0.15 * (middle + outer)

    price = np.array([cost(sizes) for sizes in cases])
    table = np.array(cases)
    fits = (table[None, :, :] >= table[:, None, :]).all(axis=2)
    paid = np.where(fits, price[None, :], 1e9)
    kept = list(range(len(cases)))
    while len(kept) > wanted:
        trials = [np.dot(paid[:, [k for k in kept if k != drop]].min(axis=1), chance) for drop in kept]
        kept.pop(int(np.argmin(trials)))
    return [cases[k] for k in sorted(kept, key=lambda k: (price[k], k))]


def pack_kernel(leaves, window, keys, values, packed, meta, choice):
    head_count = window.shape[1]
    head_dim = keys.shape[1] // head_count
    kinds = []
    for head in range(head_count):
        rows, cols = window[0, head], window[1, head]
        kinds.append(jnp.where(rows > 0, jnp.where(cols > 0, 0, 3), jnp.where(cols > 0, 1, 2)))
    for head in range(head_count):
        slot = jnp.int32(0)
        for other in range(head_count):
            if other != head:
                ahead = kinds[other] <= kinds[head] if other < head else kinds[other] < kinds[head]
                slot = slot + ahead.astype(jnp.int32)
        meta[slot] = jnp.int32(head)
        meta[head_count + slot] = kinds[head]
        columns = slice(head * head_dim, (head + 1) * head_dim)
        packed[slot, 0] = keys[:, columns]
        packed[slot, 1] = values[:, columns]
    both, cols, rows = (
        sum((kind == number).astype(jnp.int32) for kind in kinds) for number in (0, 1, 3)
    )
    best = jnp.int32(0)
    for number in reversed(range(len(leaves))):
        sizes = leaves[number]
        fits = (both <= sizes[0]) & (both + cols <= sizes[1]) & (rows <= sizes[2])
        best = jnp.where(fits, number, best)
    choice[0] = best


def attend_kernel(moves, grid_shape, order, meta, text_len, queries, keys, values, *rest):
    *blocks, out = rest
    arrived, prompts = blocks[: len(moves)], blocks[len(moves) :]
    head_count = arrived[0].shape[0]
    tile_tok = keys.shape[0]
    head_dim = keys.shape[1] // head_count
    scale = 1.0 / math.sqrt(head_dim)
    position = lax.axis_index("region")
    row, col = position // grid_shape[1], position % grid_shape[1]
    nothing = jnp.float32(-1e30)
    biases = []
    for block, owner in zip(prompts, order):
        held = block.shape[1]
        first = owner(position) * held
        tokens = first + lax.broadcasted_iota(jnp.int32, (1, held), 1)
        biases.append(jnp.where(tokens < text_len[0], jnp.float32(0), nothing))
    prompt_bias = jnp.concatenate(biases, axis=1)

    def one_slot(slot, carry):
        head = meta[slot]
        kind = meta[head_count + slot]
        columns = pl.ds(pl.multiple_of(head * head_dim, head_dim), head_dim)

        for number, reach in enumerate(KINDS):
            @pl.when(kind == number)
            def _():
                key_list = [keys[:, columns]]
                value_list = [values[:, columns]]
                bias_list = [jnp.zeros((1, tile_tok), jnp.float32)]
                for block, (row_step, col_step) in zip(arrived, moves):
                    if abs(row_step) <= reach[0] and abs(col_step) <= reach[1]:
                        key_list.append(block[slot, 0])
                        value_list.append(block[slot, 1])
                        bias = jnp.zeros((1, tile_tok), jnp.float32)
                        if grid_shape != (2, 2):
                            from_row, from_col = row - row_step, col - col_step
                            there = (from_row >= 0) & (from_row < grid_shape[0])
                            there = there & (from_col >= 0) & (from_col < grid_shape[1])
                            bias = bias + jnp.where(there, jnp.float32(0), nothing)
                        bias_list.append(bias)
                for block in prompts:
                    key_list.append(block[0, :, columns])
                    value_list.append(block[1, :, columns])
                all_keys = jnp.concatenate(key_list, axis=0)
                all_values = jnp.concatenate(value_list, axis=0)
                bias = jnp.concatenate(bias_list + [prompt_bias], axis=1)
                scores = lax.dot_general(
                    queries[:, columns], all_keys, (((1,), (1,)), ((), ())),
                    preferred_element_type=jnp.float32,
                )
                scores = scores * scale + bias
                row_max = jnp.max(scores, axis=1, keepdims=True)
                weights = jnp.exp(scores - row_max)
                row_sum = jnp.sum(weights, axis=1, keepdims=True)
                attended = jnp.dot(
                    weights.astype(jnp.bfloat16), all_values, preferred_element_type=jnp.float32
                )
                out[:, columns] = (attended / row_sum).astype(out.dtype)

        return carry

    lax.fori_loop(0, head_count, one_slot, 0)


def shards(
    video_queries, video_keys, video_values, head_window, prompt_keys, prompt_values, text_len
):
    tile_shape = video_queries.shape[2:]
    tile_tok, features = tile_shape
    head_count = head_window.shape[0]
    head_dim = features // head_count
    region_count = lax.axis_size("region")
    grid_cols = min(8, region_count // 2)
    grid_shape = (region_count // grid_cols, grid_cols)
    queries = video_queries.reshape(tile_shape)
    keys = video_keys.reshape(tile_shape)
    values = video_values.reshape(tile_shape)

    def steps(extent):
        return (0, 1) if extent == 2 else (0, 1, -1)

    moves = [(r, c) for r in steps(grid_shape[0]) for c in steps(grid_shape[1]) if r or c]

    def pairs(move):
        links = []
        for source in range(region_count):
            place = [source // grid_cols + move[0], source % grid_cols + move[1]]
            for axis in range(2):
                if grid_shape[axis] == 2:
                    place[axis] %= 2
            if 0 <= place[0] < grid_shape[0] and 0 <= place[1] < grid_cols:
                links.append((source, place[0] * grid_cols + place[1]))
        return links

    small = grid_shape == (2, 2)
    leaves = send_sizes(head_count, LEAVES) if small else [(head_count,) * 3]
    prompt_own = jnp.stack([prompt_keys, prompt_values])
    if small:
        others = [lax.ppermute(prompt_own, "region", pairs(move)) for move in moves]
        prompts = [prompt_own] + others
        order = tuple((lambda z, k=k: z ^ k) for k in range(region_count))
    else:
        prompts = [lax.all_gather(prompt_own, "region", axis=1, tiled=True)]
        order = (lambda z: 0,)
    packed, meta, choice = pl.pallas_call(
        functools.partial(pack_kernel, leaves),
        out_shape=(
            jax.ShapeDtypeStruct((head_count, 2, tile_tok, head_dim), keys.dtype),
            jax.ShapeDtypeStruct((2 * head_count,), jnp.int32),
            jax.ShapeDtypeStruct((1,), jnp.int32),
        ),
        in_specs=[SMEM, VMEM, VMEM],
        out_specs=(VMEM, SMEM, SMEM),
    )(head_window.T, keys, values)

    def exchange(sizes, packed):
        both, cols, rows = sizes

        def send(piece, move):
            return lax.ppermute(piece, "region", pairs(move)) if piece.shape[0] else piece

        def gap(count):
            return jnp.zeros((count,) + packed.shape[1:], packed.dtype)

        row_both = send(packed[:both], (1, 0))
        col_all = send(packed[:cols], (0, 1))
        row_only = send(packed[head_count - rows :], (1, 0))
        diagonal = send(row_both, (0, 1))
        return (
            jnp.concatenate([col_all, gap(head_count - cols)]),
            jnp.concatenate([row_both, gap(head_count - both - rows), row_only]),
            jnp.concatenate([diagonal, gap(head_count - both)]),
        )

    if small:
        moves = [(0, 1), (1, 0), (1, 1)]
        arrived = lax.switch(
            choice[0], [functools.partial(exchange, sizes) for sizes in leaves], packed
        )
    else:
        arrived = [lax.ppermute(packed, "region", pairs(move)) for move in moves]

    result = pl.pallas_call(
        functools.partial(attend_kernel, moves, grid_shape, order),
        out_shape=jax.ShapeDtypeStruct(tile_shape, video_queries.dtype),
        in_specs=[SMEM, SMEM] + [VMEM] * (3 + len(arrived) + len(prompts)),
        out_specs=VMEM,
        compiler_params=pltpu.CompilerParams(vmem_limit_bytes=24 * 1024 * 1024),
    )(meta, text_len, queries, keys, values, *arrived, *prompts)
    return result.reshape(video_queries.shape)


def solution(mesh):
    in_specs = (
        P("groups", "region", None, "head"),
        P("groups", "region", None, "head"),
        P("groups", "region", None, "head"),
        P("head", None),
        P(("groups", "region"), "head"),
        P(("groups", "region"), "head"),
        P("groups"),
    )
    out_specs = P("groups", "region", None, "head")
    return jax.shard_map(shards, mesh=mesh, in_specs=in_specs, out_specs=out_specs, check_vma=False)
```

```python
import functools
import math

import jax
import jax.numpy as jnp
import numpy as np
from jax import lax
from jax.experimental import pallas as pl
from jax.experimental.pallas import tpu as pltpu
from jax.sharding import PartitionSpec as P

VMEM = pl.BlockSpec(memory_space=pltpu.VMEM)
SMEM = pl.BlockSpec(memory_space=pltpu.SMEM)
KINDS = ((1, 1), (0, 1), (0, 0), (1, 0))
BOTH, COLS, NONE, ROWS = range(4)
LEAVES = 32


def send_sizes(head_count, wanted):
    span = range(head_count + 1)
    cases, chance = [], []
    for both in span:
        for cols in span[: head_count - both + 1]:
            for rows in span[: head_count - both - cols + 1]:
                parts = (both, cols, rows, head_count - both - cols - rows)
                cases.append((both, cols, both + rows))
                chance.append(1.0 / math.prod(math.factorial(part) for part in parts))

    def cost(sizes):
        middle = 4 * sizes[2]
        outer = 2 * (2 * sizes[0] + sizes[1] + sizes[2])
        return max(middle, outer) + 0.15 * (middle + outer)

    price = np.array([cost(sizes) for sizes in cases])
    table = np.array(cases)
    fits = (table[None, :, :] >= table[:, None, :]).all(axis=2)
    paid = np.where(fits, price[None, :], 1e9)
    kept = list(range(len(cases)))
    while len(kept) > wanted:
        trials = [np.dot(paid[:, [k for k in kept if k != drop]].min(axis=1), chance) for drop in kept]
        kept.pop(int(np.argmin(trials)))
    return [cases[k] for k in sorted(kept, key=lambda k: (price[k], k))]


def sort_heads(window):
    head_count = window.shape[1]
    kinds = []
    for head in range(head_count):
        rows, cols = window[0, head], window[1, head]
        along = jnp.where(cols > 0, BOTH, ROWS)
        kinds.append(jnp.where(rows > 0, along, jnp.where(cols > 0, COLS, NONE)))
    totals = [sum((kind == number).astype(jnp.int32) for kind in kinds) for number in range(4)]
    seen = [jnp.int32(0)] * 4
    seen[ROWS] = totals[BOTH]
    places = []
    for kind in kinds:
        place = jnp.int32(0)
        for number in (BOTH, COLS, ROWS):
            same = kind == number
            place = jnp.where(same, seen[number], place)
            seen[number] = seen[number] + same.astype(jnp.int32)
        places.append(place)
    return kinds, places, totals


def pack_kernel(leaves, window, keys, values, prompt_keys, prompt_values, packed, choice):
    head_count = window.shape[1]
    tile_tok = keys.shape[0]
    held = prompt_keys.shape[0]
    head_dim = keys.shape[1] // head_count
    kinds, places, totals = sort_heads(window)
    middle = head_count * 2 * tile_tok
    right = middle + head_count * 2 * held
    for head in range(head_count):
        columns = slice(head * head_dim, (head + 1) * head_dim)
        base = middle + head * 2 * held
        packed[base : base + held] = prompt_keys[:, columns]
        packed[base + held : base + 2 * held] = prompt_values[:, columns]
        slot = places[head] * (2 * tile_tok)
        start = jnp.where(kinds[head] == COLS, middle - 2 * tile_tok - slot, right + slot)

        @pl.when(kinds[head] != NONE)
        def _():
            packed[pl.ds(pl.multiple_of(start, 2 * held), tile_tok)] = keys[:, columns]
            packed[pl.ds(pl.multiple_of(start + tile_tok, 2 * held), tile_tok)] = values[:, columns]

    best = jnp.int32(0)
    for number in reversed(range(len(leaves))):
        sizes = leaves[number]
        fits = (totals[BOTH] <= sizes[0]) & (totals[COLS] <= sizes[1])
        best = jnp.where(fits & (totals[BOTH] + totals[ROWS] <= sizes[2]), number, best)
    choice[0] = best


def place_kernel(piece, out):
    rows = 256

    def some_rows(part, carry):
        lines = pl.ds(pl.multiple_of(part * rows, rows), rows)
        out[lines] = piece[lines]
        return carry

    lax.fori_loop(0, piece.shape[0] // rows, some_rows, 0)


def attend_kernel(plan, prompts, shifts, grid_shape, choice, window, text_len, *refs):
    queries, keys, values, *blocks = refs[:-3]
    out, kinds_at, places_at = refs[-3:]
    head_count = window.shape[1]
    tile_tok = queries.shape[0]
    head_dim = queries.shape[1] // head_count
    scale = 1.0 / math.sqrt(head_dim)
    nothing = jnp.float32(-1e30)
    position = lax.axis_index("region")
    row, col = position // grid_shape[1], position % grid_shape[1]
    kinds, places, _ = sort_heads(window)
    for head in range(head_count):
        kinds_at[head] = kinds[head]
        places_at[head] = places[head]
    shift = jnp.int32(0)
    for number, amount in enumerate(shifts):
        shift = jnp.where(choice[0] == number, amount, shift)
    biases = []
    for _, owner, held in prompts:
        tokens = owner(position) * held + lax.broadcasted_iota(jnp.int32, (1, held), 1)
        biases.append(jnp.where(tokens < text_len[0], jnp.float32(0), nothing))
    prompt_bias = jnp.concatenate(biases, axis=1)

    def one_head(head, carry):
        columns = pl.ds(pl.multiple_of(head * head_dim, head_dim), head_dim)

        def attend(taken):
            pairs = [(keys[:, columns], values[:, columns])]
            absent = [None]
            for (row_step, col_step), fetch in taken:
                pairs.append(fetch(blocks, head, places_at[head], columns, shift))
                from_row, from_col = row - row_step, col - col_step
                there = (from_row >= 0) & (from_row < grid_shape[0])
                there = there & (from_col >= 0) & (from_col < grid_shape[1])
                absent.append(None if grid_shape == (2, 2) else ~there)
            video = tile_tok * len(pairs)
            pairs += [fetch(blocks, head, None, columns, shift) for fetch, _, _ in prompts]
            all_keys = jnp.concatenate([pair[0] for pair in pairs], axis=0)
            all_values = jnp.concatenate([pair[1] for pair in pairs], axis=0)
            scores = lax.dot_general(
                queries[:, columns], all_keys, (((1,), (1,)), ((), ())),
                preferred_element_type=jnp.float32,
            )
            pieces = []
            for number, missing in enumerate(absent):
                piece = scores[:, tile_tok * number : tile_tok * (number + 1)]
                if missing is not None:
                    piece = piece + jnp.where(missing, nothing, jnp.float32(0))
                pieces.append(piece)
            scores = jnp.concatenate(pieces + [scores[:, video:] + prompt_bias], axis=1)
            row_max = jnp.max(scores, axis=1, keepdims=True)
            weights = jnp.exp((scores - row_max) * scale)
            row_sum = jnp.sum(weights, axis=1, keepdims=True)
            attended = jnp.dot(
                weights.astype(jnp.bfloat16), all_values, preferred_element_type=jnp.float32
            )
            out[:, columns] = (attended / row_sum).astype(out.dtype)

        for these, taken in plan:
            kind = kinds_at[head]
            pl.when(functools.reduce(jnp.logical_or, [kind == one for one in these]))(
                functools.partial(attend, taken)
            )
        return carry

    lax.fori_loop(0, head_count, one_head, 0)


def shards(
    video_queries, video_keys, video_values, head_window, prompt_keys, prompt_values, text_len
):
    tile_shape = video_queries.shape[2:]
    tile_tok, features = tile_shape
    head_count = head_window.shape[0]
    head_dim = features // head_count
    held = prompt_keys.shape[0]
    region_count = lax.axis_size("region")
    grid_cols = min(8, region_count // 2)
    grid_shape = (region_count // grid_cols, grid_cols)
    queries = video_queries.reshape(tile_shape)
    keys = video_keys.reshape(tile_shape)
    values = video_values.reshape(tile_shape)
    window = head_window.T

    def steps(extent):
        return (0, 1) if extent == 2 else (0, 1, -1)

    moves = [(r, c) for r in steps(grid_shape[0]) for c in steps(grid_shape[1]) if r or c]

    def send(piece, move):
        links = []
        for source in range(region_count):
            place = [source // grid_cols + move[0], source % grid_cols + move[1]]
            for axis in range(2):
                if grid_shape[axis] == 2:
                    place[axis] %= 2
            if 0 <= place[0] < grid_shape[0] and 0 <= place[1] < grid_cols:
                links.append((source, place[0] * grid_cols + place[1]))
        return lax.ppermute(piece, "region", links)

    def attend(plan, prompts, shifts, choice, operands):
        return pl.pallas_call(
            functools.partial(attend_kernel, plan, prompts, shifts, grid_shape),
            out_shape=jax.ShapeDtypeStruct(tile_shape, video_queries.dtype),
            in_specs=[SMEM] * 3 + [VMEM] * (len(operands) - 2),
            out_specs=VMEM,
            scratch_shapes=[pltpu.SMEM((head_count,), jnp.int32)] * 2,
            compiler_params=pltpu.CompilerParams(vmem_limit_bytes=56 * 1024 * 1024),
        )(choice, *operands)

    if grid_shape != (2, 2):

        def whole_tile(number):
            return lambda blocks, head, place, columns, shift: (
                blocks[2 * number][:, columns], blocks[2 * number + 1][:, columns],
            )

        blocks = [send(piece, move) for move in moves for piece in (keys, values)]
        prompts = ((whole_tile(len(moves)), lambda position: 0, held * region_count),)
        for piece in (prompt_keys, prompt_values):
            blocks.append(lax.all_gather(piece, "region", axis=0, tiled=True))
        plan = []
        for kind, reach in enumerate(KINDS):
            taken = [
                (move, whole_tile(number))
                for number, move in enumerate(moves)
                if abs(move[0]) <= reach[0] and abs(move[1]) <= reach[1]
            ]
            plan.append(((kind,), tuple(taken)))
        operands = (window, text_len, queries, keys, values, *blocks)
        return attend(plan, prompts, (), text_len, operands).reshape(video_queries.shape)

    leaves = send_sizes(head_count, LEAVES)
    slot_rows, prompt_rows = 2 * tile_tok, 2 * held * head_count
    middle = head_count * slot_rows
    right = middle + prompt_rows
    packed, choice = pl.pallas_call(
        functools.partial(pack_kernel, leaves),
        out_shape=(
            jax.ShapeDtypeStruct((right + middle, head_dim), keys.dtype),
            jax.ShapeDtypeStruct((1,), jnp.int32),
        ),
        in_specs=[SMEM] + [VMEM] * 4,
        out_specs=(VMEM, SMEM),
    )(window, keys, values, prompt_keys, prompt_values)

    def leaf(sizes, packed):
        both, cols, rows = sizes
        along_rows = send(packed[middle : right + rows * slot_rows], (1, 0))
        along_cols = send(
            packed[middle - cols * slot_rows : right + both * slot_rows], (0, 1)
        )
        diagonal = send(along_rows[: prompt_rows + both * slot_rows], (0, 1))

        def full(piece):
            return pl.pallas_call(
                place_kernel,
                out_shape=pltpu.VMEM((prompt_rows + middle, head_dim), piece.dtype),
                in_specs=[VMEM],
                out_specs=VMEM,
                compiler_params=pltpu.CompilerParams(vmem_limit_bytes=4 * 1024 * 1024),
            )(piece)

        return full(along_rows), full(along_cols), full(diagonal)

    arrived = lax.switch(choice[0], [functools.partial(leaf, sizes) for sizes in leaves], packed)

    def block_of(number, from_end, count):
        def fetch(blocks, head, place, columns, shift):
            start = (shift if number == 1 else 0) + (0 if place is None else prompt_rows)
            if place is None:
                base = start + head * 2 * held
            elif from_end:
                base = shift - (place + 1) * slot_rows
            else:
                base = start + place * slot_rows
            base = pl.multiple_of(base, 2 * held)
            return blocks[number][pl.ds(base, count)], blocks[number][pl.ds(base + count, count)]

        return fetch

    def own_prompt(blocks, head, place, columns, shift):
        return blocks[3][:, columns], blocks[4][:, columns]

    from_rows = ((1, 0), block_of(0, False, tile_tok))
    from_cols = ((0, 1), block_of(1, False, tile_tok))
    from_both = ((1, 1), block_of(2, False, tile_tok))
    plan = (
        ((BOTH,), (from_rows, from_cols, from_both)),
        ((COLS,), (((0, 1), block_of(1, True, tile_tok)),)),
        ((NONE,), ()),
        ((ROWS,), (from_rows,)),
    )
    prompts = [(own_prompt, lambda position: position, held)]
    for number, flip in enumerate((2, 1, 3)):
        prompts.append((block_of(number, False, held), lambda position, k=flip: position ^ k, held))
    shifts = [sizes[1] * slot_rows for sizes in leaves]
    operands = (window, text_len, queries, keys, values, *arrived, prompt_keys, prompt_values)
    return attend(plan, prompts, shifts, choice, operands).reshape(video_queries.shape)


def solution(mesh):
    in_specs = (
        P("groups", "region", None, "head"),
        P("groups", "region", None, "head"),
        P("groups", "region", None, "head"),
        P("head", None),
        P(("groups", "region"), "head"),
        P(("groups", "region"), "head"),
        P("groups"),
    )
    out_specs = P("groups", "region", None, "head")
    return jax.shard_map(shards, mesh=mesh, in_specs=in_specs, out_specs=out_specs, check_vma=False)
```

```python
import functools
import math

import jax
import jax.numpy as jnp
import numpy as np
from jax import lax
from jax.experimental import pallas as pl
from jax.experimental.pallas import tpu as pltpu
from jax.sharding import PartitionSpec as P

VMEM = pl.BlockSpec(memory_space=pltpu.VMEM)
SMEM = pl.BlockSpec(memory_space=pltpu.SMEM)
ANY = pl.BlockSpec(memory_space=pl.ANY)
KINDS = ((1, 1), (0, 1), (0, 0), (1, 0))
BOTH, COLS, NONE, ROWS = range(4)
LEAVES = 32
AT_ONCE = 3


def send_sizes(head_count, wanted):
    span = range(head_count + 1)
    cases, chance = [], []
    for both in span:
        for cols in span[: head_count - both + 1]:
            for rows in span[: head_count - both - cols + 1]:
                parts = (both, cols, rows, head_count - both - cols - rows)
                cases.append((both, cols, both + rows))
                chance.append(1.0 / math.prod(math.factorial(part) for part in parts))

    def cost(sizes):
        middle = 4 * sizes[2]
        outer = 2 * (sizes[0] + sizes[1] + sizes[2])
        return max(middle, outer) + 2 * sizes[0] + 0.15 * (middle + outer)

    price = np.array([cost(sizes) for sizes in cases])
    table = np.array(cases)
    fits = (table[None, :, :] >= table[:, None, :]).all(axis=2)
    paid = np.where(fits, price[None, :], 1e9)
    kept = list(range(len(cases)))
    while len(kept) > wanted:
        trials = [np.dot(paid[:, [k for k in kept if k != drop]].min(axis=1), chance) for drop in kept]
        kept.pop(int(np.argmin(trials)))
    return [cases[k] for k in sorted(kept, key=lambda k: (price[k], k))]


def sort_heads(window):
    head_count = window.shape[1]
    kinds = []
    for head in range(head_count):
        rows, cols = window[0, head], window[1, head]
        along = jnp.where(cols > 0, BOTH, ROWS)
        kinds.append(jnp.where(rows > 0, along, jnp.where(cols > 0, COLS, NONE)))
    totals = [sum((kind == number).astype(jnp.int32) for kind in kinds) for number in range(4)]
    seen = [jnp.int32(0)] * 4
    seen[ROWS] = totals[BOTH]
    places = []
    for kind in kinds:
        place = jnp.int32(0)
        for number in (BOTH, COLS, ROWS):
            same = kind == number
            place = jnp.where(same, seen[number], place)
            seen[number] = seen[number] + same.astype(jnp.int32)
        places.append(place)
    return kinds, places, totals


def pack_kernel(leaves, window, far_text, keys, values, prompt_keys, prompt_values, packed, choice, meta, text_len, sem):
    text_copy = pltpu.make_async_copy(far_text, text_len, sem)
    text_copy.start()
    head_count = window.shape[1]
    tile_tok = keys.shape[0]
    held = prompt_keys.shape[0]
    head_dim = keys.shape[1] // head_count
    kinds, places, totals = sort_heads(window)
    middle = head_count * 2 * tile_tok
    right = middle + head_count * 2 * held
    for head in range(head_count):
        columns = slice(head * head_dim, (head + 1) * head_dim)
        base = middle + head * 2 * held
        packed[base : base + held] = prompt_keys[:, columns]
        packed[base + held : base + 2 * held] = prompt_values[:, columns]
        slot = places[head] * (2 * tile_tok)
        start = jnp.where(kinds[head] == COLS, middle - 2 * tile_tok - slot, right + slot)

        @pl.when(kinds[head] != NONE)
        def _():
            packed[pl.ds(pl.multiple_of(start, 2 * held), tile_tok)] = keys[:, columns]
            packed[pl.ds(pl.multiple_of(start + tile_tok, 2 * held), tile_tok)] = values[:, columns]

    best, sent = jnp.int32(0), jnp.int32(0)
    for number in reversed(range(len(leaves))):
        sizes = leaves[number]
        fits = (totals[BOTH] <= sizes[0]) & (totals[COLS] <= sizes[1])
        fits = fits & (totals[BOTH] + totals[ROWS] <= sizes[2])
        best = jnp.where(fits, number, best)
        sent = jnp.where(fits, sizes[1], sent)
    choice[0] = best
    text_copy.wait()
    write_meta(meta, kinds, places, sent, text_len)


def write_meta(meta, kinds, places, sent, text_len):
    for head, (kind, place) in enumerate(zip(kinds, places)):
        meta[2 * head] = kind
        meta[2 * head + 1] = place
    meta[2 * len(kinds)] = sent
    meta[2 * len(kinds) + 1] = text_len[0]


def meta_kernel(window, text_len, meta):
    kinds, places, _ = sort_heads(window)
    write_meta(meta, kinds, places, jnp.int32(0), text_len)


def place_kernel(piece, out):
    rows = 256

    def some_rows(part, carry):
        lines = pl.ds(pl.multiple_of(part * rows, rows), rows)
        out[lines] = piece[lines]
        return carry

    lax.fori_loop(0, piece.shape[0] // rows, some_rows, 0)


def attend_kernel(tiles, prompts, grid_shape, head_dim, meta, *refs):
    queries, keys, values, *blocks, out = refs
    head_count = meta.shape[0] // 2 - 1
    tile_tok = queries.shape[0]
    at_once = queries.shape[1] // head_dim
    scale = 1.0 / math.sqrt(head_dim)
    nothing = jnp.float32(-1e30)
    position = lax.axis_index("region")
    row, col = position // grid_shape[1], position % grid_shape[1]
    shift = meta[2 * head_count] * (2 * tile_tok)
    biases = []
    for _, owner, held in prompts:
        tokens = owner(position) * held + lax.broadcasted_iota(jnp.int32, (1, held), 1)
        biases.append(jnp.where(tokens < meta[2 * head_count + 1], jnp.float32(0), nothing))
    prompt_bias = jnp.concatenate(biases, axis=1)
    all_columns, all_scores, all_values = [], [], []
    for number in range(at_once):
        head = pl.program_id(0) * at_once + number
        kind, place = meta[2 * head], meta[2 * head + 1]
        columns = slice(number * head_dim, (number + 1) * head_dim)
        pairs, masks = [(keys[:, columns], values[:, columns])], [None]
        for (row_step, col_step), readers, fetch in tiles:
            reads = functools.reduce(jnp.logical_or, [kind == reader for reader in readers])
            pairs.append(fetch(blocks, head, columns, kind, place, reads, shift))
            if grid_shape != (2, 2):
                from_row, from_col = row - row_step, col - col_step
                reads = reads & (from_row >= 0) & (from_row < grid_shape[0])
                reads = reads & (from_col >= 0) & (from_col < grid_shape[1])
            masks.append(jnp.where(reads, jnp.float32(0), nothing))
        video = tile_tok * len(pairs)
        pairs += [fetch(blocks, head, columns, shift) for fetch, _, _ in prompts]
        scores = lax.dot_general(
            queries[:, columns],
            jnp.concatenate([pair[0] for pair in pairs], axis=0),
            (((1,), (1,)), ((), ())),
            preferred_element_type=jnp.float32,
        )
        pieces = []
        for tile, mask in enumerate(masks):
            piece = scores[:, tile_tok * tile : tile_tok * (tile + 1)]
            pieces.append(piece if mask is None else piece + mask)
        all_scores.append(jnp.concatenate(pieces + [scores[:, video:] + prompt_bias], axis=1))
        all_values.append(jnp.concatenate([pair[1] for pair in pairs], axis=0))
        all_columns.append(columns)
    row_maxes = [jnp.max(scores, axis=1, keepdims=True) for scores in all_scores]
    weights = [jnp.exp((s - m) * scale) for s, m in zip(all_scores, row_maxes)]
    row_sums = [jnp.sum(w, axis=1, keepdims=True) for w in weights]
    attended = [
        jnp.dot(w.astype(jnp.bfloat16), v, preferred_element_type=jnp.float32)
        for w, v in zip(weights, all_values)
    ]
    for columns, total, summed in zip(all_columns, row_sums, attended):
        out[:, columns] = (summed / total).astype(out.dtype)


def shards(
    video_queries, video_keys, video_values, head_window, prompt_keys, prompt_values, text_len
):
    tile_shape = video_queries.shape[2:]
    tile_tok, features = tile_shape
    head_count = head_window.shape[0]
    head_dim = features // head_count
    held = prompt_keys.shape[0]
    region_count = lax.axis_size("region")
    grid_cols = min(8, region_count // 2)
    grid_shape = (region_count // grid_cols, grid_cols)
    queries = video_queries.reshape(tile_shape)
    keys = video_keys.reshape(tile_shape)
    values = video_values.reshape(tile_shape)
    window = head_window.T

    def steps(extent):
        return (0, 1) if extent == 2 else (0, 1, -1)

    moves = [(r, c) for r in steps(grid_shape[0]) for c in steps(grid_shape[1]) if r or c]

    def send(piece, move):
        links = []
        for source in range(region_count):
            place = [source // grid_cols + move[0], source % grid_cols + move[1]]
            for axis in range(2):
                if grid_shape[axis] == 2:
                    place[axis] %= 2
            if 0 <= place[0] < grid_shape[0] and 0 <= place[1] < grid_cols:
                links.append((source, place[0] * grid_cols + place[1]))
        return lax.ppermute(piece, "region", links)

    at_once = max(count for count in range(1, AT_ONCE + 1) if head_count % count == 0)

    def attend(tiles, prompts, meta, own, arrived):
        def by_heads(piece):
            return pl.BlockSpec((piece.shape[0], at_once * head_dim), lambda step: (0, step))

        whole = VMEM if grid_shape == (2, 2) else None
        return pl.pallas_call(
            functools.partial(attend_kernel, tiles, prompts, grid_shape, head_dim),
            grid=(head_count // at_once,),
            out_shape=jax.ShapeDtypeStruct(tile_shape, video_queries.dtype),
            in_specs=[SMEM]
            + [by_heads(piece) for piece in own]
            + [whole or by_heads(piece) for piece in arrived],
            out_specs=by_heads(queries),
            compiler_params=pltpu.CompilerParams(vmem_limit_bytes=56 * 1024 * 1024),
        )(meta, *own, *arrived)

    if grid_shape != (2, 2):

        def whole_tile(number):
            return lambda blocks, head, columns, *_: (
                blocks[2 * number][:, columns], blocks[2 * number + 1][:, columns],
            )

        blocks = [send(piece, move) for move in moves for piece in (keys, values)]
        prompts = ((whole_tile(len(moves)), lambda position: 0, held * region_count),)
        for piece in (prompt_keys, prompt_values):
            blocks.append(lax.all_gather(piece, "region", axis=0, tiled=True))
        tiles = []
        for number, move in enumerate(moves):
            readers = [
                kind
                for kind, reach in enumerate(KINDS)
                if abs(move[0]) <= reach[0] and abs(move[1]) <= reach[1]
            ]
            tiles.append((move, readers, whole_tile(number)))
        meta = pl.pallas_call(
            meta_kernel,
            out_shape=jax.ShapeDtypeStruct((2 * head_count + 2,), jnp.int32),
            in_specs=[SMEM, SMEM],
            out_specs=SMEM,
        )(window, text_len)
        own = (queries, keys, values)
        return attend(tiles, prompts, meta, own, blocks).reshape(video_queries.shape)

    leaves = send_sizes(head_count, LEAVES)
    slot_rows, prompt_rows = 2 * tile_tok, 2 * held * head_count
    middle = head_count * slot_rows
    right = middle + prompt_rows
    packed, choice, meta = pl.pallas_call(
        functools.partial(pack_kernel, leaves),
        out_shape=(
            jax.ShapeDtypeStruct((right + middle, head_dim), keys.dtype),
            jax.ShapeDtypeStruct((1,), jnp.int32),
            jax.ShapeDtypeStruct((2 * head_count + 2,), jnp.int32),
        ),
        in_specs=[SMEM, ANY] + [VMEM] * 4,
        out_specs=(VMEM, SMEM, SMEM),
        scratch_shapes=[pltpu.SMEM((1,), jnp.int32), pltpu.SemaphoreType.DMA],
    )(window, text_len, keys, values, prompt_keys, prompt_values)

    def leaf(sizes, packed):
        both, cols, rows = sizes
        along_rows = send(packed[middle : right + rows * slot_rows], (1, 0))
        along_cols = send(
            packed[middle - cols * slot_rows : right + both * slot_rows], (0, 1)
        )
        diagonal = send(along_rows[: prompt_rows + both * slot_rows], (0, 1))

        def full(piece):
            return pl.pallas_call(
                place_kernel,
                out_shape=pltpu.VMEM((prompt_rows + middle, head_dim), piece.dtype),
                in_specs=[VMEM],
                out_specs=VMEM,
                compiler_params=pltpu.CompilerParams(vmem_limit_bytes=4 * 1024 * 1024),
            )(piece)

        return full(along_rows), full(along_cols), full(diagonal)

    arrived = lax.switch(choice[0], [functools.partial(leaf, sizes) for sizes in leaves], packed)

    def start_of(number, shift):
        return shift if number == 1 else 0

    def tile_of(number):
        def fetch(blocks, head, columns, kind, place, reads, shift):
            start = start_of(number, shift)
            base = jnp.where(reads, start + prompt_rows + place * slot_rows, start)
            if number == 1:
                base = jnp.where(kind == COLS, start - (place + 1) * slot_rows, base)
            base = pl.multiple_of(base, 2 * held)
            block = blocks[2 + number]
            return block[pl.ds(base, tile_tok)], block[pl.ds(base + tile_tok, tile_tok)]

        return fetch

    def prompt_of(number):
        def fetch(blocks, head, columns, shift):
            base = pl.multiple_of(start_of(number, shift) + head * 2 * held, 2 * held)
            block = blocks[2 + number]
            return block[pl.ds(base, held)], block[pl.ds(base + held, held)]

        return fetch

    def own_prompt(blocks, head, columns, shift):
        return blocks[0][:, columns], blocks[1][:, columns]

    tiles = (
        ((1, 0), (BOTH, ROWS), tile_of(0)),
        ((0, 1), (BOTH, COLS), tile_of(1)),
        ((1, 1), (BOTH,), tile_of(2)),
    )
    prompts = [(own_prompt, lambda position: position, held)]
    for number, flip in enumerate((2, 1, 3)):
        prompts.append((prompt_of(number), lambda position, k=flip: position ^ k, held))
    own = (queries, keys, values, prompt_keys, prompt_values)
    return attend(tiles, prompts, meta, own, arrived).reshape(video_queries.shape)


def solution(mesh):
    in_specs = (
        P("groups", "region", None, "head"),
        P("groups", "region", None, "head"),
        P("groups", "region", None, "head"),
        P("head", None),
        P(("groups", "region"), "head"),
        P(("groups", "region"), "head"),
        P("groups"),
    )
    out_specs = P("groups", "region", None, "head")
    return jax.shard_map(shards, mesh=mesh, in_specs=in_specs, out_specs=out_specs, check_vma=False)
```

```python
import functools
import math

import jax
import jax.numpy as jnp
import numpy as np
from jax import lax
from jax.experimental import pallas as pl
from jax.experimental.pallas import tpu as pltpu
from jax.sharding import PartitionSpec as P

VMEM = pl.BlockSpec(memory_space=pltpu.VMEM)
SMEM = pl.BlockSpec(memory_space=pltpu.SMEM)
KINDS = ((1, 1), (0, 1), (0, 0), (1, 0))
BOTH, COLS, NONE, ROWS = range(4)
LEAVES = 32
AT_ONCE = 3


def send_sizes(head_count, wanted):
    span = range(head_count + 1)
    cases, chance = [], []
    for both in span:
        for cols in span[: head_count - both + 1]:
            for rows in span[: head_count - both - cols + 1]:
                parts = (both, cols, rows, head_count - both - cols - rows)
                cases.append((both, cols, both + rows))
                chance.append(1.0 / math.prod(math.factorial(part) for part in parts))

    def cost(sizes):
        middle = 4 * sizes[2]
        outer = 2 * (sizes[0] + sizes[1] + sizes[2])
        return max(middle, outer) + 2 * sizes[0] + 0.15 * (middle + outer)

    price = np.array([cost(sizes) for sizes in cases])
    table = np.array(cases)
    fits = (table[None, :, :] >= table[:, None, :]).all(axis=2)
    paid = np.where(fits, price[None, :], 1e9)
    kept = list(range(len(cases)))
    while len(kept) > wanted:
        trials = [np.dot(paid[:, [k for k in kept if k != drop]].min(axis=1), chance) for drop in kept]
        kept.pop(int(np.argmin(trials)))
    return [cases[k] for k in sorted(kept, key=lambda k: (price[k], k))]


def sort_heads(window):
    head_count = window.shape[1]
    kinds = []
    for head in range(head_count):
        rows, cols = window[0, head], window[1, head]
        along = jnp.where(cols > 0, BOTH, ROWS)
        kinds.append(jnp.where(rows > 0, along, jnp.where(cols > 0, COLS, NONE)))
    totals = [sum((kind == number).astype(jnp.int32) for kind in kinds) for number in range(4)]
    seen = [jnp.int32(0)] * 4
    seen[ROWS] = totals[BOTH]
    places = []
    for kind in kinds:
        place = jnp.int32(0)
        for number in (BOTH, COLS, ROWS):
            same = kind == number
            place = jnp.where(same, seen[number], place)
            seen[number] = seen[number] + same.astype(jnp.int32)
        places.append(place)
    return kinds, places, totals


def pack_kernel(leaves, window, keys, values, prompt_keys, prompt_values, packed, choice, meta):
    head_count = window.shape[1]
    tile_tok = keys.shape[0]
    held = prompt_keys.shape[0]
    head_dim = keys.shape[1] // head_count
    kinds, places, totals = sort_heads(window)
    middle = head_count * 2 * tile_tok
    right = middle + head_count * 2 * held
    for head in range(head_count):
        columns = slice(head * head_dim, (head + 1) * head_dim)
        base = middle + head * 2 * held
        packed[base : base + held] = prompt_keys[:, columns]
        packed[base + held : base + 2 * held] = prompt_values[:, columns]
        slot = places[head] * (2 * tile_tok)
        start = jnp.where(kinds[head] == COLS, middle - 2 * tile_tok - slot, right + slot)

        @pl.when(kinds[head] != NONE)
        def _():
            packed[pl.ds(pl.multiple_of(start, 2 * held), tile_tok)] = keys[:, columns]
            packed[pl.ds(pl.multiple_of(start + tile_tok, 2 * held), tile_tok)] = values[:, columns]

    best, sent = jnp.int32(0), jnp.int32(0)
    for number in reversed(range(len(leaves))):
        sizes = leaves[number]
        fits = (totals[BOTH] <= sizes[0]) & (totals[COLS] <= sizes[1])
        fits = fits & (totals[BOTH] + totals[ROWS] <= sizes[2])
        best = jnp.where(fits, number, best)
        sent = jnp.where(fits, sizes[1], sent)
    choice[0] = best
    write_meta(meta, kinds, places, sent)


def write_meta(meta, kinds, places, sent):
    for head, (kind, place) in enumerate(zip(kinds, places)):
        meta[2 * head] = kind
        meta[2 * head + 1] = place
    meta[2 * len(kinds)] = sent


def meta_kernel(window, text_len, meta):
    kinds, places, _ = sort_heads(window)
    write_meta(meta, kinds, places, jnp.int32(0))
    meta[2 * len(kinds) + 1] = text_len[0]


def place_kernel(pieces, *refs):
    first = 0
    for piece in refs[:pieces]:
        place_rows(piece, refs[-1], first)
        first += piece.shape[0]
    if len(refs) > pieces + 1:
        meta, text_len, longer = refs[pieces : pieces + 3]
        for number in range(meta.shape[0]):
            longer[number] = meta[number]
        longer[meta.shape[0]] = text_len[0]


def place_rows(piece, out, first):
    rows = 256

    def some_rows(part, carry):
        source = pl.ds(pl.multiple_of(part * rows, rows), rows)
        target = pl.ds(pl.multiple_of(first + part * rows, rows), rows)
        out[target] = piece[source]
        return carry

    lax.fori_loop(0, piece.shape[0] // rows, some_rows, 0)


def attend_kernel(tiles, prompts, grid_shape, head_dim, meta, *refs):
    queries, keys, values, *blocks, out = refs
    head_count = meta.shape[0] // 2 - 1
    tile_tok = queries.shape[0]
    at_once = queries.shape[1] // head_dim
    scale = 1.0 / math.sqrt(head_dim)
    nothing = jnp.float32(-1e30)
    position = lax.axis_index("region")
    row, col = position // grid_shape[1], position % grid_shape[1]
    shift = meta[2 * head_count] * (2 * tile_tok)
    biases = []
    for _, owner, held in prompts:
        tokens = owner(position) * held + lax.broadcasted_iota(jnp.int32, (1, held), 1)
        biases.append(jnp.where(tokens < meta[2 * head_count + 1], jnp.float32(0), nothing))
    prompt_bias = jnp.concatenate(biases, axis=1)
    all_columns, all_scores, all_values = [], [], []
    for number in range(at_once):
        head = pl.program_id(0) * at_once + number
        kind, place = meta[2 * head], meta[2 * head + 1]
        columns = slice(number * head_dim, (number + 1) * head_dim)
        pairs, masks = [(keys[:, columns], values[:, columns])], [None]
        for (row_step, col_step), readers, fetch in tiles:
            reads = functools.reduce(jnp.logical_or, [kind == reader for reader in readers])
            pairs.append(fetch(blocks, head, columns, kind, place, reads, shift))
            if grid_shape != (2, 2):
                from_row, from_col = row - row_step, col - col_step
                reads = reads & (from_row >= 0) & (from_row < grid_shape[0])
                reads = reads & (from_col >= 0) & (from_col < grid_shape[1])
            masks.append(jnp.where(reads, jnp.float32(0), nothing))
        video = tile_tok * len(pairs)
        pairs += [fetch(blocks, head, columns, shift) for fetch, _, _ in prompts]
        scores = lax.dot_general(
            queries[:, columns],
            jnp.concatenate([pair[0] for pair in pairs], axis=0),
            (((1,), (1,)), ((), ())),
            preferred_element_type=jnp.float32,
        )
        pieces = []
        for tile, mask in enumerate(masks):
            piece = scores[:, tile_tok * tile : tile_tok * (tile + 1)]
            pieces.append(piece if mask is None else piece + mask)
        all_scores.append(jnp.concatenate(pieces + [scores[:, video:] + prompt_bias], axis=1))
        all_values.append(jnp.concatenate([pair[1] for pair in pairs], axis=0))
        all_columns.append(columns)
    row_maxes = [jnp.max(scores, axis=1, keepdims=True) for scores in all_scores]
    weights = [jnp.exp((s - m) * scale) for s, m in zip(all_scores, row_maxes)]
    row_sums = [jnp.sum(w, axis=1, keepdims=True) for w in weights]
    attended = [
        jnp.dot(w.astype(jnp.bfloat16), v, preferred_element_type=jnp.float32)
        for w, v in zip(weights, all_values)
    ]
    for columns, total, summed in zip(all_columns, row_sums, attended):
        out[:, columns] = (summed / total).astype(out.dtype)


def shards(
    video_queries, video_keys, video_values, head_window, prompt_keys, prompt_values, text_len
):
    tile_shape = video_queries.shape[2:]
    tile_tok, features = tile_shape
    head_count = head_window.shape[0]
    head_dim = features // head_count
    held = prompt_keys.shape[0]
    region_count = lax.axis_size("region")
    grid_cols = min(8, region_count // 2)
    grid_shape = (region_count // grid_cols, grid_cols)
    queries = video_queries.reshape(tile_shape)
    keys = video_keys.reshape(tile_shape)
    values = video_values.reshape(tile_shape)
    window = head_window.T

    def steps(extent):
        return (0, 1) if extent == 2 else (0, 1, -1)

    moves = [(r, c) for r in steps(grid_shape[0]) for c in steps(grid_shape[1]) if r or c]

    def send(piece, move):
        links = []
        for source in range(region_count):
            place = [source // grid_cols + move[0], source % grid_cols + move[1]]
            for axis in range(2):
                if grid_shape[axis] == 2:
                    place[axis] %= 2
            if 0 <= place[0] < grid_shape[0] and 0 <= place[1] < grid_cols:
                links.append((source, place[0] * grid_cols + place[1]))
        return lax.ppermute(piece, "region", links)

    at_once = max(count for count in range(1, AT_ONCE + 1) if head_count % count == 0)

    def attend(tiles, prompts, meta, own, arrived):
        def by_heads(piece):
            return pl.BlockSpec((piece.shape[0], at_once * head_dim), lambda step: (0, step))

        whole = VMEM if grid_shape == (2, 2) else None
        return pl.pallas_call(
            functools.partial(attend_kernel, tiles, prompts, grid_shape, head_dim),
            grid=(head_count // at_once,),
            out_shape=jax.ShapeDtypeStruct(tile_shape, video_queries.dtype),
            in_specs=[SMEM]
            + [by_heads(piece) for piece in own]
            + [whole or by_heads(piece) for piece in arrived],
            out_specs=by_heads(queries),
            compiler_params=pltpu.CompilerParams(vmem_limit_bytes=56 * 1024 * 1024),
        )(meta, *own, *arrived)

    if grid_shape != (2, 2):

        def whole_tile(number):
            return lambda blocks, head, columns, *_: (
                blocks[2 * number][:, columns], blocks[2 * number + 1][:, columns],
            )

        blocks = [send(piece, move) for move in moves for piece in (keys, values)]
        prompts = ((whole_tile(len(moves)), lambda position: 0, held * region_count),)
        for piece in (prompt_keys, prompt_values):
            blocks.append(lax.all_gather(piece, "region", axis=0, tiled=True))
        tiles = []
        for number, move in enumerate(moves):
            readers = [
                kind
                for kind, reach in enumerate(KINDS)
                if abs(move[0]) <= reach[0] and abs(move[1]) <= reach[1]
            ]
            tiles.append((move, readers, whole_tile(number)))
        meta = pl.pallas_call(
            meta_kernel,
            out_shape=jax.ShapeDtypeStruct((2 * head_count + 2,), jnp.int32),
            in_specs=[SMEM, SMEM],
            out_specs=SMEM,
        )(window, text_len)
        own = (queries, keys, values)
        return attend(tiles, prompts, meta, own, blocks).reshape(video_queries.shape)

    leaves = send_sizes(head_count, LEAVES)
    slot_rows, prompt_rows = 2 * tile_tok, 2 * held * head_count
    middle = head_count * slot_rows
    right = middle + prompt_rows
    packed, choice, meta = pl.pallas_call(
        functools.partial(pack_kernel, leaves),
        out_shape=(
            jax.ShapeDtypeStruct((right + middle, head_dim), keys.dtype),
            jax.ShapeDtypeStruct((1,), jnp.int32),
            jax.ShapeDtypeStruct((2 * head_count + 1,), jnp.int32),
        ),
        in_specs=[SMEM] + [VMEM] * 4,
        out_specs=(VMEM, SMEM, SMEM),
    )(window, keys, values, prompt_keys, prompt_values)

    def full(*pieces, scalar=()):
        out = pltpu.VMEM((prompt_rows + middle, head_dim), packed.dtype)
        count = jax.ShapeDtypeStruct((2 * head_count + 2,), jnp.int32)
        return pl.pallas_call(
            functools.partial(place_kernel, len(pieces)),
            out_shape=(count, out) if scalar else out,
            in_specs=[VMEM] * len(pieces) + [SMEM] * len(scalar),
            out_specs=(SMEM, VMEM) if scalar else VMEM,
            compiler_params=pltpu.CompilerParams(vmem_limit_bytes=4 * 1024 * 1024),
        )(*pieces, *scalar)

    def leaf(sizes, packed, meta, text_len):
        both, cols, rows = sizes
        middle_end = right + both * slot_rows
        along_rows = send(packed[middle : right + rows * slot_rows], (1, 0))
        along_cols = send(packed[middle - cols * slot_rows : middle_end], (0, 1))
        diagonal = send(along_rows[: prompt_rows + both * slot_rows], (0, 1))
        meta, along_cols = full(along_cols, scalar=(meta, text_len))
        return meta, full(along_rows), along_cols, full(diagonal)

    meta, *arrived = lax.switch(
        choice[0], [functools.partial(leaf, sizes) for sizes in leaves], packed, meta, text_len
    )

    def start_of(number, shift):
        return shift if number == 1 else 0

    def tile_of(number):
        def fetch(blocks, head, columns, kind, place, reads, shift):
            start = start_of(number, shift)
            base = jnp.where(reads, start + prompt_rows + place * slot_rows, start)
            if number == 1:
                base = jnp.where(kind == COLS, start - (place + 1) * slot_rows, base)
            base = pl.multiple_of(base, 2 * held)
            block = blocks[2 + number]
            return block[pl.ds(base, tile_tok)], block[pl.ds(base + tile_tok, tile_tok)]

        return fetch

    def prompt_of(number):
        def fetch(blocks, head, columns, shift):
            base = pl.multiple_of(start_of(number, shift) + head * 2 * held, 2 * held)
            block = blocks[2 + number]
            return block[pl.ds(base, held)], block[pl.ds(base + held, held)]

        return fetch

    def own_prompt(blocks, head, columns, shift):
        return blocks[0][:, columns], blocks[1][:, columns]

    tiles = (
        ((1, 0), (BOTH, ROWS), tile_of(0)),
        ((0, 1), (BOTH, COLS), tile_of(1)),
        ((1, 1), (BOTH,), tile_of(2)),
    )
    prompts = [(own_prompt, lambda position: position, held)]
    for number, flip in enumerate((2, 1, 3)):
        prompts.append((prompt_of(number), lambda position, k=flip: position ^ k, held))
    own = (queries, keys, values, prompt_keys, prompt_values)
    return attend(tiles, prompts, meta, own, arrived).reshape(video_queries.shape)


def solution(mesh):
    in_specs = (
        P("groups", "region", None, "head"),
        P("groups", "region", None, "head"),
        P("groups", "region", None, "head"),
        P("head", None),
        P(("groups", "region"), "head"),
        P(("groups", "region"), "head"),
        P("groups"),
    )
    out_specs = P("groups", "region", None, "head")
    return jax.shard_map(shards, mesh=mesh, in_specs=in_specs, out_specs=out_specs, check_vma=False)
```

```python
import functools
import math

import jax
import jax.numpy as jnp
import numpy as np
from jax import lax
from jax.experimental import pallas as pl
from jax.experimental.pallas import tpu as pltpu
from jax.sharding import PartitionSpec as P

VMEM = pl.BlockSpec(memory_space=pltpu.VMEM)
SMEM = pl.BlockSpec(memory_space=pltpu.SMEM)
KINDS = ((1, 1), (0, 1), (0, 0), (1, 0))
BOTH, COLS, NONE, ROWS = range(4)
LEAVES = 32
AT_ONCE = 3


def send_sizes(head_count, wanted):
    span = range(head_count + 1)
    cases, chance = [], []
    for both in span:
        for cols in span[: head_count - both + 1]:
            for rows in span[: head_count - both - cols + 1]:
                parts = (both, cols, rows, head_count - both - cols - rows)
                cases.append((both, cols, both + rows))
                chance.append(1.0 / math.prod(math.factorial(part) for part in parts))

    def cost(sizes):
        middle = 4 * sizes[2]
        outer = 2 * (sizes[0] + sizes[1] + sizes[2])
        return max(middle, outer) + 2 * sizes[0] + 0.15 * (middle + outer)

    price = np.array([cost(sizes) for sizes in cases])
    table = np.array(cases)
    fits = (table[None, :, :] >= table[:, None, :]).all(axis=2)
    paid = np.where(fits, price[None, :], 1e9)
    kept = list(range(len(cases)))
    while len(kept) > wanted:
        trials = [np.dot(paid[:, [k for k in kept if k != drop]].min(axis=1), chance) for drop in kept]
        kept.pop(int(np.argmin(trials)))
    return [cases[k] for k in sorted(kept, key=lambda k: (price[k], k))]


def sort_heads(window):
    head_count = window.shape[1]
    kinds = []
    for head in range(head_count):
        rows, cols = window[0, head], window[1, head]
        along = jnp.where(cols > 0, BOTH, ROWS)
        kinds.append(jnp.where(rows > 0, along, jnp.where(cols > 0, COLS, NONE)))
    totals = [sum((kind == number).astype(jnp.int32) for kind in kinds) for number in range(4)]
    seen = [jnp.int32(0)] * 4
    seen[ROWS] = totals[BOTH]
    places = []
    for kind in kinds:
        place = jnp.int32(0)
        for number in (BOTH, COLS, ROWS):
            same = kind == number
            place = jnp.where(same, seen[number], place)
            seen[number] = seen[number] + same.astype(jnp.int32)
        places.append(place)
    return kinds, places, totals


def pack_kernel(leaves, window, keys, values, prompt_keys, prompt_values, packed, choice, meta):
    head_count = window.shape[1]
    tile_tok = keys.shape[0]
    held = prompt_keys.shape[0]
    head_dim = keys.shape[1] // head_count
    kinds, places, totals = sort_heads(window)
    middle = head_count * 2 * tile_tok
    right = middle + head_count * 2 * held
    for head in range(head_count):
        columns = slice(head * head_dim, (head + 1) * head_dim)
        base = middle + head * 2 * held
        packed[base : base + held] = prompt_keys[:, columns]
        packed[base + held : base + 2 * held] = prompt_values[:, columns]
        slot = places[head] * (2 * tile_tok)
        start = jnp.where(kinds[head] == COLS, middle - 2 * tile_tok - slot, right + slot)

        @pl.when(kinds[head] != NONE)
        def _():
            packed[pl.ds(pl.multiple_of(start, 2 * held), tile_tok)] = keys[:, columns]
            packed[pl.ds(pl.multiple_of(start + tile_tok, 2 * held), tile_tok)] = values[:, columns]

    best, sent = jnp.int32(0), jnp.int32(0)
    for number in reversed(range(len(leaves))):
        sizes = leaves[number]
        fits = (totals[BOTH] <= sizes[0]) & (totals[COLS] <= sizes[1])
        fits = fits & (totals[BOTH] + totals[ROWS] <= sizes[2])
        best = jnp.where(fits, number, best)
        sent = jnp.where(fits, sizes[1], sent)
    choice[0] = best
    write_meta(meta, kinds, places, sent)


def write_meta(meta, kinds, places, sent):
    for head, (kind, place) in enumerate(zip(kinds, places)):
        meta[2 * head] = kind
        meta[2 * head + 1] = place
    meta[2 * len(kinds)] = sent


def meta_kernel(window, text_len, meta):
    kinds, places, _ = sort_heads(window)
    write_meta(meta, kinds, places, jnp.int32(0))
    meta[2 * len(kinds) + 1] = text_len[0]


def place_kernel(pieces, *refs):
    first = 0
    for piece in refs[:pieces]:
        place_rows(piece, refs[-1], first)
        first += piece.shape[0]
    if len(refs) > pieces + 1:
        meta, text_len, longer = refs[pieces : pieces + 3]
        for number in range(meta.shape[0]):
            longer[number] = meta[number]
        longer[meta.shape[0]] = text_len[0]


def place_rows(piece, out, first):
    rows = 256

    def some_rows(part, carry):
        source = pl.ds(pl.multiple_of(part * rows, rows), rows)
        target = pl.ds(pl.multiple_of(first + part * rows, rows), rows)
        out[target] = piece[source]
        return carry

    lax.fori_loop(0, piece.shape[0] // rows, some_rows, 0)


def attend_kernel(tiles, prompts, grid_shape, head_dim, meta, *refs):
    queries, keys, values, *blocks, out = refs
    head_count = meta.shape[0] // 2 - 1
    tile_tok = queries.shape[0]
    at_once = queries.shape[1] // head_dim
    scale = math.log2(math.e) / math.sqrt(head_dim)
    nothing = jnp.float32(-1e30)
    position = lax.axis_index("region")
    row, col = position // grid_shape[1], position % grid_shape[1]
    shift = meta[2 * head_count] * (2 * tile_tok)
    biases = []
    for _, owner, held in prompts:
        tokens = owner(position) * held + lax.broadcasted_iota(jnp.int32, (1, held), 1)
        biases.append(jnp.where(tokens < meta[2 * head_count + 1], jnp.float32(0), nothing))
    prompt_bias = jnp.concatenate(biases, axis=1)
    all_columns, all_scores, all_values = [], [], []
    for number in range(at_once):
        head = pl.program_id(0) * at_once + number
        kind, place = meta[2 * head], meta[2 * head + 1]
        columns = slice(number * head_dim, (number + 1) * head_dim)
        pairs, masks = [(keys[:, columns], values[:, columns])], [None]
        for (row_step, col_step), readers, fetch in tiles:
            reads = functools.reduce(jnp.logical_or, [kind == reader for reader in readers])
            pairs.append(fetch(blocks, head, columns, kind, place, reads, shift))
            if grid_shape != (2, 2):
                from_row, from_col = row - row_step, col - col_step
                reads = reads & (from_row >= 0) & (from_row < grid_shape[0])
                reads = reads & (from_col >= 0) & (from_col < grid_shape[1])
            masks.append(jnp.where(reads, jnp.float32(0), nothing))
        video = tile_tok * len(pairs)
        pairs += [fetch(blocks, head, columns, shift) for fetch, _, _ in prompts]
        scores = lax.dot_general(
            queries[:, columns],
            jnp.concatenate([pair[0] for pair in pairs], axis=0),
            (((1,), (1,)), ((), ())),
            preferred_element_type=jnp.float32,
        )
        pieces = []
        for tile, mask in enumerate(masks):
            piece = scores[:, tile_tok * tile : tile_tok * (tile + 1)]
            pieces.append(piece if mask is None else piece + mask)
        all_scores.append(jnp.concatenate(pieces + [scores[:, video:] + prompt_bias], axis=1))
        all_values.append(jnp.concatenate([pair[1] for pair in pairs], axis=0))
        all_columns.append(columns)
    row_maxes = [jnp.max(scores, axis=1, keepdims=True) for scores in all_scores]
    weights = [jnp.exp2((s - m) * scale) for s, m in zip(all_scores, row_maxes)]
    row_sums = [jnp.sum(w, axis=1, keepdims=True) for w in weights]
    attended = [
        jnp.dot(w.astype(jnp.bfloat16), v, preferred_element_type=jnp.float32)
        for w, v in zip(weights, all_values)
    ]
    for columns, total, summed in zip(all_columns, row_sums, attended):
        out[:, columns] = (summed / total).astype(out.dtype)


def shards(
    video_queries, video_keys, video_values, head_window, prompt_keys, prompt_values, text_len
):
    tile_shape = video_queries.shape[2:]
    tile_tok, features = tile_shape
    head_count = head_window.shape[0]
    head_dim = features // head_count
    held = prompt_keys.shape[0]
    region_count = lax.axis_size("region")
    grid_cols = min(8, region_count // 2)
    grid_shape = (region_count // grid_cols, grid_cols)
    queries = video_queries.reshape(tile_shape)
    keys = video_keys.reshape(tile_shape)
    values = video_values.reshape(tile_shape)
    window = head_window.T

    def steps(extent):
        return (0, 1) if extent == 2 else (0, 1, -1)

    moves = [(r, c) for r in steps(grid_shape[0]) for c in steps(grid_shape[1]) if r or c]

    def send(piece, move):
        links = []
        for source in range(region_count):
            place = [source // grid_cols + move[0], source % grid_cols + move[1]]
            for axis in range(2):
                if grid_shape[axis] == 2:
                    place[axis] %= 2
            if 0 <= place[0] < grid_shape[0] and 0 <= place[1] < grid_cols:
                links.append((source, place[0] * grid_cols + place[1]))
        return lax.ppermute(piece, "region", links)

    at_once = max(count for count in range(1, AT_ONCE + 1) if head_count % count == 0)

    def attend(tiles, prompts, meta, own, arrived):
        def by_heads(piece):
            return pl.BlockSpec((piece.shape[0], at_once * head_dim), lambda step: (0, step))

        whole = VMEM if grid_shape == (2, 2) else None
        return pl.pallas_call(
            functools.partial(attend_kernel, tiles, prompts, grid_shape, head_dim),
            grid=(head_count // at_once,),
            out_shape=jax.ShapeDtypeStruct(tile_shape, video_queries.dtype),
            in_specs=[SMEM]
            + [by_heads(piece) for piece in own]
            + [whole or by_heads(piece) for piece in arrived],
            out_specs=by_heads(queries),
            compiler_params=pltpu.CompilerParams(vmem_limit_bytes=56 * 1024 * 1024),
        )(meta, *own, *arrived)

    if grid_shape != (2, 2):

        def whole_tile(number):
            return lambda blocks, head, columns, *_: (
                blocks[2 * number][:, columns], blocks[2 * number + 1][:, columns],
            )

        blocks = [send(piece, move) for move in moves for piece in (keys, values)]
        prompts = ((whole_tile(len(moves)), lambda position: 0, held * region_count),)
        for piece in (prompt_keys, prompt_values):
            blocks.append(lax.all_gather(piece, "region", axis=0, tiled=True))
        tiles = []
        for number, move in enumerate(moves):
            readers = [
                kind
                for kind, reach in enumerate(KINDS)
                if abs(move[0]) <= reach[0] and abs(move[1]) <= reach[1]
            ]
            tiles.append((move, readers, whole_tile(number)))
        meta = pl.pallas_call(
            meta_kernel,
            out_shape=jax.ShapeDtypeStruct((2 * head_count + 2,), jnp.int32),
            in_specs=[SMEM, SMEM],
            out_specs=SMEM,
        )(window, text_len)
        own = (queries, keys, values)
        return attend(tiles, prompts, meta, own, blocks).reshape(video_queries.shape)

    leaves = send_sizes(head_count, LEAVES)
    slot_rows, prompt_rows = 2 * tile_tok, 2 * held * head_count
    middle = head_count * slot_rows
    right = middle + prompt_rows
    packed, choice, meta = pl.pallas_call(
        functools.partial(pack_kernel, leaves),
        out_shape=(
            jax.ShapeDtypeStruct((right + middle, head_dim), keys.dtype),
            jax.ShapeDtypeStruct((1,), jnp.int32),
            jax.ShapeDtypeStruct((2 * head_count + 1,), jnp.int32),
        ),
        in_specs=[SMEM] + [VMEM] * 4,
        out_specs=(VMEM, SMEM, SMEM),
    )(window, keys, values, prompt_keys, prompt_values)

    def full(*pieces, scalar=()):
        out = pltpu.VMEM((prompt_rows + middle, head_dim), packed.dtype)
        count = jax.ShapeDtypeStruct((2 * head_count + 2,), jnp.int32)
        return pl.pallas_call(
            functools.partial(place_kernel, len(pieces)),
            out_shape=(count, out) if scalar else out,
            in_specs=[VMEM] * len(pieces) + [SMEM] * len(scalar),
            out_specs=(SMEM, VMEM) if scalar else VMEM,
            compiler_params=pltpu.CompilerParams(vmem_limit_bytes=4 * 1024 * 1024),
        )(*pieces, *scalar)

    def leaf(sizes, packed, meta, text_len):
        both, cols, rows = sizes
        middle_end = right + both * slot_rows
        along_rows = send(packed[middle : right + rows * slot_rows], (1, 0))
        along_cols = send(packed[middle - cols * slot_rows : middle_end], (0, 1))
        diagonal = send(along_rows[: prompt_rows + both * slot_rows], (0, 1))
        meta, along_cols = full(along_cols, scalar=(meta, text_len))
        return meta, full(along_rows), along_cols, full(diagonal)

    meta, *arrived = lax.switch(
        choice[0], [functools.partial(leaf, sizes) for sizes in leaves], packed, meta, text_len
    )

    def start_of(number, shift):
        return shift if number == 1 else 0

    def tile_of(number):
        def fetch(blocks, head, columns, kind, place, reads, shift):
            start = start_of(number, shift)
            base = jnp.where(reads, start + prompt_rows + place * slot_rows, start)
            if number == 1:
                base = jnp.where(kind == COLS, start - (place + 1) * slot_rows, base)
            base = pl.multiple_of(base, 2 * held)
            block = blocks[2 + number]
            return block[pl.ds(base, tile_tok)], block[pl.ds(base + tile_tok, tile_tok)]

        return fetch

    def prompt_of(number):
        def fetch(blocks, head, columns, shift):
            base = pl.multiple_of(start_of(number, shift) + head * 2 * held, 2 * held)
            block = blocks[2 + number]
            return block[pl.ds(base, held)], block[pl.ds(base + held, held)]

        return fetch

    def own_prompt(blocks, head, columns, shift):
        return blocks[0][:, columns], blocks[1][:, columns]

    tiles = (
        ((1, 0), (BOTH, ROWS), tile_of(0)),
        ((0, 1), (BOTH, COLS), tile_of(1)),
        ((1, 1), (BOTH,), tile_of(2)),
    )
    prompts = [(own_prompt, lambda position: position, held)]
    for number, flip in enumerate((2, 1, 3)):
        prompts.append((prompt_of(number), lambda position, k=flip: position ^ k, held))
    own = (queries, keys, values, prompt_keys, prompt_values)
    return attend(tiles, prompts, meta, own, arrived).reshape(video_queries.shape)


def solution(mesh):
    in_specs = (
        P("groups", "region", None, "head"),
        P("groups", "region", None, "head"),
        P("groups", "region", None, "head"),
        P("head", None),
        P(("groups", "region"), "head"),
        P(("groups", "region"), "head"),
        P("groups"),
    )
    out_specs = P("groups", "region", None, "head")
    return jax.shard_map(shards, mesh=mesh, in_specs=in_specs, out_specs=out_specs, check_vma=False)
```
